32 devices in a mesh: ctx: 8 (over z, x), tp: 4 (over y, core).
Axes of the slice: x: 2, y: 2, z: 4, core: 2. Of those that a mesh axis runs over, the one named last changes fastest.
Arguments:
- tokens: bfloat16 [2048, 8192], P('ctx'), may hold values from -6 to 6
- select_index: int32 [256], P('ctx'), may hold values from 0 to 255, as said below
- valid_count: int32 [8], replicated, may hold values from 4 to 32, as said below
- queries: bfloat16 [256, 4096], P('ctx', 'tp'), may hold values from -160 to 160
- key_matrix: bfloat16 [8192, 512], P('ctx', 'tp'), may hold values from -0.0625 to 0.0625
- value_matrix: bfloat16 [8192, 512], P('ctx', 'tp'), may hold values from -0.0625 to 0.0625
- out_grad: bfloat16 [256, 4096], P('ctx', 'tp'), may hold values from -6 to 6
Outputs:
- attended: bfloat16 [256, 4096], P('ctx', 'tp')
- query_gradient: bfloat16 [256, 4096], P('ctx', 'tp')
- token_grad: bfloat16 [2048, 8192], P('ctx', 'tp')
- key_weight_grad: bfloat16 [8192, 512], P('ctx', 'tp')
- value_weight_grad: bfloat16 [8192, 512], P('ctx', 'tp')
The draws below stay inside these ranges and needn't reach their ends.
Inputs may be any that keep to these rules, and one draw needn't show every extreme that they name: `select_index`: within one shard the offsets of all 32 slots are distinct, and those of the first valid_count slots rise. `valid_count`: some shard holds exactly 32 live slots.
All inputs are finite; a program needn't handle non-finite values.
Results may differ from the reference program's by a relative error of at most 0.023.
The reference program's roundings to bfloat16 on the way count: a program that leaves them out, or rounds other values in their place, can miss the bound.
Values may be sent and summed in bfloat16 or wider, within the bound.
No kernel may reach another device: no remote copies, remote signals or barrier semaphores. Data moves between devices by JAX's collectives and lax.ppermute only.
A program may use at most 64 MiB of HBM per device.

```python
import math
import jax
import jax.numpy as jnp
from jax import lax

MODEL_WIDTH = 8192
HEAD_WIDTH = 128
KEY_VALUE_HEADS = 4
HEADS_PER_KEY = 8
SHARD = 256
SLOT_LIMIT = 32
HQ = 32
SEQ = 2048
ROUTED_KEYS = 256


def draw_order(subkey):
    return jax.random.permutation(subkey, SHARD)


def selection(key):
    shards = ROUTED_KEYS // SLOT_LIMIT
    counts = jax.random.randint(jax.random.fold_in(key, 11), (shards,), SLOT_LIMIT // 8, 3 * SLOT_LIMIT // 4 + 1)
    busiest = jax.random.randint(jax.random.fold_in(key, 12), (), 0, shards)
    counts = jnp.where(jnp.arange(shards) == busiest, SLOT_LIMIT, counts).astype(jnp.int32)
    subkeys = jax.random.split(jax.random.fold_in(key, 13), shards)
    orders = jax.vmap(draw_order)(subkeys)[:, :SLOT_LIMIT].astype(jnp.int32)
    is_live = jnp.arange(SLOT_LIMIT)[None, :] < counts[:, None]
    ranked = jnp.sort(jnp.where(is_live, orders, orders + SHARD), axis=1)
    offsets = jnp.where(ranked >= SHARD, ranked - SHARD, ranked)
    return (counts, offsets.reshape(ROUTED_KEYS).astype(jnp.int32))


def draw_valid_count(key, part):
    return selection(key)[0]


def draw_select_index(key, part):
    return selection(key)[1]


def draw_queries(key, part):
    random_perturb = jax.random.normal(jax.random.fold_in(key, 21), (ROUTED_KEYS, KEY_VALUE_HEADS * HEADS_PER_KEY * HEAD_WIDTH), jnp.float32)
    random_perturb = jnp.clip(random_perturb, -6.0, 6.0)
    return random_perturb.astype(jnp.bfloat16)


def levels(own_key, extent, cuts, least, top_value):
    def one(dim, blocks):
        draws = jax.random.uniform(jax.random.fold_in(jax.random.fold_in(own_key, 6), dim), (blocks,), jnp.float32, least / len(cuts), top_value / len(cuts))
        return jnp.repeat(jnp.exp(draws), extent[dim] // blocks).reshape((-1,) + (1,) * (len(extent) - dim - 1))

    loudness = one(*cuts[0])
    for cut in cuts[1:]:
        loudness = loudness * one(*cut)
    return loudness


def centred(own_key, dims, scale, limit, cuts=(), kind=jnp.bfloat16):
    values = jax.random.normal(own_key, dims, jnp.float32) * scale
    if len(cuts) > 0:
        values = levels(own_key, dims, cuts, -0.22, 0.18) * values
    return jnp.clip(values, min=-limit, max=limit).astype(kind)


def setup_inputs(seed: int = 0) -> dict:
    key_of = jax.random.split(jax.random.key(seed), 8)
    tokens = centred(key_of[0], (SEQ, MODEL_WIDTH), 1.0, 6.0, ((0, 8),))
    select_index = draw_select_index(jax.random.fold_in(key_of[7], 71), 0)
    valid_count = draw_valid_count(jax.random.fold_in(key_of[7], 71), 0)
    queries = draw_queries(jax.random.fold_in(key_of[7], 71), 0)
    key_matrix = centred(key_of[4], (MODEL_WIDTH, KEY_VALUE_HEADS * HEAD_WIDTH), MODEL_WIDTH ** -0.5, 0.0625, ((0, 8), (1, 4)))
    value_matrix = centred(key_of[5], (MODEL_WIDTH, KEY_VALUE_HEADS * HEAD_WIDTH), MODEL_WIDTH ** -0.5, 0.0625, ((0, 8), (1, 4)))
    out_grad = centred(key_of[6], (ROUTED_KEYS, HQ * HEAD_WIDTH), 1.0, 6.0, ((0, 8), (1, 4)))
    return {"tokens": tokens, "select_index": select_index, "valid_count": valid_count, "queries": queries, "key_matrix": key_matrix, "value_matrix": value_matrix, "out_grad": out_grad}


def reference(tokens, select_index, valid_count, queries, key_matrix, value_matrix, out_grad):
    score_scale = 1.0 / math.sqrt(HEAD_WIDTH)
    key_value_width = KEY_VALUE_HEADS * HEAD_WIDTH
    key_ids = jnp.arange(ROUTED_KEYS, dtype=jnp.int32)
    key_shard = key_ids // SLOT_LIMIT
    slot_in = key_ids % SLOT_LIMIT
    key_live = slot_in < jnp.take(valid_count, key_shard)
    row_ids = (key_shard * SHARD + select_index).astype(jnp.int32)
    query_pos = jnp.where(key_live, row_ids, key_shard * SHARD + SHARD)
    picked = jnp.take(tokens, row_ids, axis=0)
    key_vectors = jnp.dot(picked, key_matrix, preferred_element_type=jnp.float32).astype(jnp.bfloat16)
    value_vectors = jnp.dot(picked, value_matrix, preferred_element_type=jnp.float32).astype(jnp.bfloat16)
    heads_of_key = key_vectors.astype(jnp.float32).reshape(ROUTED_KEYS, KEY_VALUE_HEADS, HEAD_WIDTH)
    heads_of_value = value_vectors.astype(jnp.float32).reshape(ROUTED_KEYS, KEY_VALUE_HEADS, HEAD_WIDTH)
    gradient_rows = jnp.where(key_live[:, None], out_grad, jnp.zeros_like(out_grad))

    def per_shard(carried, shard):
        key_accumulator, value_accumulator = carried
        leading_item = (shard * SLOT_LIMIT).astype(jnp.int32)
        query_block = lax.dynamic_slice_in_dim(queries, leading_item, SLOT_LIMIT, 0).astype(jnp.float32).reshape(SLOT_LIMIT, KEY_VALUE_HEADS, HEADS_PER_KEY, HEAD_WIDTH)
        gradient_block = lax.dynamic_slice_in_dim(gradient_rows, leading_item, SLOT_LIMIT, 0).astype(jnp.float32).reshape(SLOT_LIMIT, KEY_VALUE_HEADS, HEADS_PER_KEY, HEAD_WIDTH)
        live_blk = lax.dynamic_slice_in_dim(key_live, leading_item, SLOT_LIMIT, 0)
        pos_blk = lax.dynamic_slice_in_dim(query_pos, leading_item, SLOT_LIMIT, 0)
        visible = key_live[None, :] & (row_ids[None, :] <= pos_blk[:, None])
        scores = jnp.einsum('qkgd,nkd->kgqn', query_block, heads_of_key) * score_scale
        scores = jnp.where(visible[None, None], scores, -jnp.inf)
        log_total = jax.nn.logsumexp(scores, axis=-1)
        probs = jnp.exp(scores - log_total[..., None])
        weight_matrices = lax.optimization_barrier(probs.astype(jnp.bfloat16)).astype(jnp.float32)
        output_single = jnp.einsum('kgqn,nkd->qkgd', weight_matrices, heads_of_value)
        output_single = jnp.where(live_blk[:, None, None, None], output_single, 0.0).astype(jnp.bfloat16)
        out_dot = jnp.transpose(lax.optimization_barrier(jnp.sum(gradient_block * output_single.astype(jnp.float32), axis=-1)), (1, 2, 0))
        grad_probs = jnp.einsum('qkgd,nkd->kgqn', gradient_block, heads_of_value)
        score_gradient = probs * (grad_probs - out_dot[..., None]) * score_scale
        score_gradient = lax.optimization_barrier(score_gradient.astype(jnp.bfloat16)).astype(jnp.float32)
        query_gradient = jnp.einsum('kgqn,nkd->qkgd', score_gradient, heads_of_key).astype(jnp.bfloat16)
        key_accumulator = key_accumulator + jnp.einsum('kgqn,qkgd->nkd', score_gradient, query_block)
        value_accumulator = value_accumulator + jnp.einsum('kgqn,qkgd->nkd', weight_matrices, gradient_block)
        return ((key_accumulator, value_accumulator), (output_single.reshape(SLOT_LIMIT, KEY_VALUE_HEADS * HEADS_PER_KEY * HEAD_WIDTH), query_gradient.reshape(SLOT_LIMIT, KEY_VALUE_HEADS * HEADS_PER_KEY * HEAD_WIDTH)))
    empty_accumulator = jnp.zeros((ROUTED_KEYS, KEY_VALUE_HEADS, HEAD_WIDTH), jnp.float32)
    (key_accumulator, value_accumulator), (output_rows, query_gradient_rows) = lax.scan(per_shard, (empty_accumulator, empty_accumulator), jnp.arange(ROUTED_KEYS // SLOT_LIMIT, dtype=jnp.int32))
    attended = output_rows.reshape(ROUTED_KEYS, KEY_VALUE_HEADS * HEADS_PER_KEY * HEAD_WIDTH)
    query_gradient = query_gradient_rows.reshape(ROUTED_KEYS, KEY_VALUE_HEADS * HEADS_PER_KEY * HEAD_WIDTH)
    key_grads = key_accumulator.reshape(ROUTED_KEYS, key_value_width).astype(jnp.bfloat16)
    value_grads = value_accumulator.reshape(ROUTED_KEYS, key_value_width).astype(jnp.bfloat16)
    key_weight_grad = jnp.dot(picked.T, key_grads, preferred_element_type=jnp.float32).astype(jnp.bfloat16)
    value_weight_grad = jnp.dot(picked.T, value_grads, preferred_element_type=jnp.float32).astype(jnp.bfloat16)
    row_grad = jnp.dot(key_grads, key_matrix.T, preferred_element_type=jnp.float32) + jnp.dot(value_grads, value_matrix.T, preferred_element_type=jnp.float32)
    row_grad = jnp.where(key_live[:, None], row_grad, 0.0)
    token_grad = jnp.zeros(tokens.shape, jnp.float32).at[row_ids].set(row_grad).astype(jnp.bfloat16)
    return (attended, query_gradient, token_grad, key_weight_grad, value_weight_grad)
```

```python
import functools
import math

import jax
import jax.numpy as jnp
from jax import lax
from jax.experimental import pallas as pl
from jax.experimental.pallas import tpu as pltpu
from jax.sharding import PartitionSpec as P

HEAD = 128
NEG = -1e30
HIDDEN = 1 << 30
F32 = jnp.float32
BF16 = jnp.bfloat16


VMEM = pl.BlockSpec(memory_space=pltpu.VMEM)
SMEM = pl.BlockSpec(memory_space=pltpu.SMEM)
HBM = pl.BlockSpec(memory_space=pltpu.HBM)


def dot(x, y, cx, cy):
    return lax.dot_general(x, y, (((cx,), (cy,)), ((), ())), preferred_element_type=F32)


def place(inner):
    ctx = lax.axis_index("ctx")
    return ctx // inner, lax.rem(ctx, inner), lax.axis_index("tp")


def call(body, outs, in_specs, out_specs, scratch=(), cost=None, name=None):
    return pl.pallas_call(
        body,
        out_shape=outs,
        in_specs=in_specs,
        out_specs=out_specs,
        scratch_shapes=list(scratch),
        compiler_params=pltpu.CompilerParams(vmem_limit_bytes=48 * 2**20),
        cost_estimate=cost,
        name=name,
    )


def cost(flops, nbytes):
    return pl.CostEstimate(flops=int(flops), bytes_accessed=int(nbytes), transcendentals=0)


def one_hot(select_ref, limit, rows, width):
    at = lax.broadcasted_iota(jnp.int32, (rows, width), 0)
    wanted = jnp.full((rows, width), -1, jnp.int32)
    for j in range(rows):
        wanted = jnp.where((at == j) & (j < limit), select_ref[j], wanted)
    column = lax.broadcasted_iota(jnp.int32, (rows, width), 1)
    return jnp.where(column == wanted, 1.0, 0.0).astype(BF16)


def pick_body(
    size, inner, half, select_hbm, count_hbm, tokens_ref, q_ref, og_ref, k_ref, v_ref, *rest
):
    pairs = size // 2 - 1
    outs, (qd_ref, w_ref, hot_ref) = rest[: pairs + 2], rest[pairs + 2 : pairs + 5]
    select_ref, count_ref, buf, sems, side = rest[pairs + 5 :]
    a, b, t = place(inner)
    cap, rows = outs[0].shape[0], tokens_ref.shape[0]
    width = q_ref.shape[1]
    core = lax.rem(t, 2)
    first = [
        pltpu.make_async_copy(select_hbm, select_ref, side.at[0]),
        pltpu.make_async_copy(count_hbm, count_ref, side.at[1]),
    ]
    for c in first:
        c.start()
    starts = [(a ^ (2 * i + 1 + core)) * (2 * half) for i in range(pairs)]
    starts += [(a ^ (size - 1)) * (2 * half) + core * half, a * (2 * half)]
    copies = []
    for i, at in enumerate(starts):
        wide = outs[i].shape[1]
        copies.append(
            pltpu.make_async_copy(
                tokens_ref.at[:, pl.ds(pl.multiple_of(at, 128), wide)],
                buf.at[:, 2 * half * i : 2 * half * i + wide],
                sems.at[i],
            )
        )
        copies[i].start()
    others = [
        pltpu.make_async_copy(q_ref, qd_ref.at[:, :width], side.at[2]),
        pltpu.make_async_copy(og_ref, qd_ref.at[:, width:], side.at[3]),
        pltpu.make_async_copy(k_ref, w_ref.at[:, : k_ref.shape[1]], side.at[4]),
        pltpu.make_async_copy(v_ref, w_ref.at[:, k_ref.shape[1] :], side.at[5]),
    ]
    for c in others:
        c.start()
    for c in first:
        c.wait()
    hot = one_hot(select_ref, cap, cap, rows)
    slot = lax.broadcasted_iota(jnp.int32, (cap, rows), 0)
    live = slot < count_ref[a * inner + b]
    hot_ref[...] = jnp.where(live, hot.astype(F32), 0.0).astype(BF16)
    for i in range(len(starts)):
        copies[i].wait()
        wide = outs[i].shape[1]
        outs[i][...] = dot(hot, buf[:, 2 * half * i : 2 * half * i + wide], 1, 0).astype(BF16)
    for c in others:
        c.wait()


def project_body(size, inner, half, *refs):
    pairs = size // 2 - 1
    got, other_ref, own_ref, w_ref = refs[: pairs + 1], refs[pairs + 1], refs[pairs + 2], refs[pairs + 3]
    kv_refs = refs[pairs + 4 : pairs + 2 * inner + 2]
    outs = refs[pairs + 2 * inner + 2 :]
    part_ref, cols, ws, rows_ref = outs[0], outs[1 : inner + 1], outs[inner + 1 : 2 * inner], outs[-1]
    a, b, t = place(inner)
    cap = own_ref.shape[0]
    core = lax.rem(t, 2)

    def to(z):
        return pl.ds(pl.multiple_of(z * cap, cap), cap)

    def side(k):
        return pl.ds(pl.multiple_of(k * half, 128), half)

    rows_ref[to(a), :] = own_ref[...]
    for i in range(pairs):
        rows_ref[to(a ^ (2 * i + 1 + core)), :] = got[i][...]
        rows_ref[to(a ^ (2 * i + 2 - core)), :] = other_ref[:, 2 * half * i : 2 * half * (i + 1)]
    rows_ref[to(a ^ (size - 1)), side(core)] = got[pairs][...]
    rows_ref[to(a ^ (size - 1)), side(1 - core)] = other_ref[:, 2 * half * pairs :]
    depth, kv_width = w_ref.shape[0], w_ref.shape[1] // 2
    total = None
    for s in range(inner):
        part = rows_ref[:, pl.ds(pl.multiple_of((b ^ s) * depth, 128), depth)]
        cols[s][...] = part
        if s:
            ws[s - 1][:, :kv_width] = kv_refs[2 * s - 2][...]
            ws[s - 1][:, kv_width:] = kv_refs[2 * s - 1][...]
        term = dot(part, (ws[s - 1] if s else w_ref)[...], 1, 0)
        total = term if total is None else total + term
    part_ref[...] = total.astype(BF16)


def attend_body(size, inner, cap, group, count_ref, *refs):
    qds, kvs = refs[:size], refs[size : size + inner]
    att_ref, dq_ref = refs[size + inner : size + inner + 2]
    kept_ref = refs[size + inner + 2]
    sent = refs[size + inner + 3 : size + 2 * inner + 2]
    q_all, do_all = refs[size + 2 * inner + 2 :]
    a, b, t = place(inner)
    width = group * HEAD
    block = group * cap
    scale = 1.0 / math.sqrt(HEAD)
    slot = lax.broadcasted_iota(jnp.int32, (cap, HEAD), 0)
    for s in range(size):
        count = count_ref[(a ^ s) * inner + b]
        for g in range(group):
            to = slice(s * block + g * cap, s * block + (g + 1) * cap)
            q_all[to, :] = qds[s][:, g * HEAD : (g + 1) * HEAD]
            rows = qds[s][:, width + g * HEAD : width + (g + 1) * HEAD]
            do_all[to, :] = jnp.where(slot < count, rows.astype(F32), 0.0).astype(BF16)
    kv = jnp.concatenate([r[...] for r in kvs], axis=0)
    keys, values = kv[:, :HEAD], kv[:, HEAD:]
    keys_t = keys.astype(F32).T.astype(BF16)
    values_t = values.astype(F32).T.astype(BF16)
    row = lax.broadcasted_iota(jnp.int32, (cap, block), 0)
    pieces = []
    for s in range(inner):
        for z in range(size):
            shard = z * inner + (b ^ s)
            pieces.append(jnp.where(row < count_ref[shard], shard * cap + row, HIDDEN))
    key_at = jnp.concatenate(pieces, axis=0)
    column = lax.rem(lax.broadcasted_iota(jnp.int32, (1, block), 1), cap)
    dk = dv = None
    for s in range(size):
        shard = (a ^ s) * inner + b
        live = column < count_ref[shard]
        q = q_all[s * block : (s + 1) * block, :]
        do = do_all[s * block : (s + 1) * block, :]
        scores = dot(keys, q, 1, 1) * scale
        scores = jnp.where(key_at <= shard * cap + column, scores, NEG)
        terms = jnp.exp(scores - jnp.max(scores, axis=0, keepdims=True))
        probs = terms * (1.0 / jnp.sum(terms, axis=0, keepdims=True))
        weights = probs.astype(BF16)
        att = jnp.where(live, dot(values_t, weights, 1, 0), 0.0).astype(BF16).astype(F32)
        do_t = do.astype(F32).T
        out_dot = jnp.sum(do_t * att, axis=0, keepdims=True)
        grad_probs = dot(values, do, 1, 1)
        grad_scores = (probs * (grad_probs - out_dot) * scale).astype(BF16)
        k_term, v_term = dot(grad_scores, q, 1, 0), dot(weights, do, 1, 0)
        dk = k_term if dk is None else dk + k_term
        dv = v_term if dv is None else dv + v_term
        if s == 0:
            att_rows = att.T.astype(BF16)
            dq_rows = dot(keys_t, grad_scores, 1, 0).T.astype(BF16)
            for g in range(group):
                att_ref[:, g * HEAD : (g + 1) * HEAD] = att_rows[g * cap : (g + 1) * cap, :]
                dq_ref[:, g * HEAD : (g + 1) * HEAD] = dq_rows[g * cap : (g + 1) * cap, :]
    rows = size * cap
    kept_ref[:, :HEAD] = dk[:rows, :]
    kept_ref[:, HEAD:] = dv[:rows, :]
    for s in range(1, inner):
        sent[s - 1][:, :HEAD] = dk[s * rows : (s + 1) * rows, :].astype(BF16)
        sent[s - 1][:, HEAD:] = dv[s * rows : (s + 1) * rows, :].astype(BF16)


def total_body(inner, *refs):
    terms, grads_ref = refs[:inner], refs[inner]
    total = terms[0][...]
    for r in terms[1:]:
        total = total + r[...].astype(F32)
    grads_ref[...] = total.astype(BF16)


def total_pieces_body(size, inner, cap, *refs):
    total_body(inner, *refs[: inner + 1])
    grads_ref, low_ref, high_ref = refs[inner:]
    t = lax.axis_index("tp")
    for s in range(size):
        u = t ^ s
        at = lax.rem(u, 2) * (size // 2) + u // 2
        piece = grads_ref[pl.ds(pl.multiple_of(at * cap, cap), cap), :]
        out_ref, j = (low_ref, s) if s < size // 2 else (high_ref, s - size // 2)
        out_ref[j * cap : (j + 1) * cap, :] = piece


def weight_body(inner, *refs):
    cols, grads, (k_ref, v_ref) = refs[:inner], refs[inner : 2 * inner], refs[2 * inner :]
    total = None
    for c, g in zip(cols, grads):
        term = dot(c[...], g[...], 0, 0)
        total = term if total is None else total + term
    width = k_ref.shape[1]
    k_ref[...] = total[:, :width].astype(BF16)
    v_ref[...] = total[:, width:].astype(BF16)


def rows_body(size, inner, *refs):
    grads, weights, out_ref = refs[:size], refs[size : size + size * inner], refs[-1]
    a, b, t = place(inner)
    depth = weights[0].shape[0]
    for j in range(inner):
        total = None
        for s in range(size):
            term = dot(grads[s][...], weights[s * inner + j][...], 1, 1)
            total = term if total is None else total + term
        out_ref[:, pl.ds(pl.multiple_of((b ^ j) * depth, 128), depth)] = total.astype(BF16)


def scatter_body(hot_ref, rows_ref, out_ref):
    out_ref[...] = dot(hot_ref[...], rows_ref[...], 0, 0).astype(BF16)


def after(x, *others):
    return lax.optimization_barrier((x, *others))[0]


def local(tokens, select_index, valid_count, queries, key_matrix, value_matrix, out_grad):
    size, ctx = lax.axis_size("tp"), lax.axis_size("ctx")
    inner = ctx // size
    cap = select_index.shape[0]
    rows, model = tokens.shape
    depth, kv_width = key_matrix.shape
    width = queries.shape[1]
    group = width // kv_width
    half = inner * depth // 2
    slots = size * cap
    pairs = size // 2 - 1
    shape = jax.ShapeDtypeStruct

    def a_swap(x, s):
        return lax.ppermute(x, "ctx", [(j, (j // inner ^ s) * inner + j % inner) for j in range(ctx)])

    def b_swap(x, s):
        return lax.ppermute(x, "ctx", [(j, j // inner * inner + (j % inner ^ s)) for j in range(ctx)])

    def t_swap(x, s):
        return lax.ppermute(x, "tp", [(j, j ^ s) for j in range(size)])

    def move(x, target):
        index = [(a, b, t) for a in range(size) for b in range(inner) for t in range(size)]
        flat = lambda a, b, t: (a * inner + b) * size + t
        return lax.ppermute(x, ("ctx", "tp"), [(flat(*i), flat(*target(*i))) for i in index])

    kv_swapped = [b_swap(x, s) for s in range(1, inner) for x in (key_matrix, value_matrix)]

    *picked, own, qd, weights, hot = call(
        functools.partial(pick_body, size, inner, half),
        [shape((cap, 2 * half), BF16)] * pairs
        + [shape((cap, half), BF16), shape((cap, 2 * half), BF16)]
        + [shape((cap, 2 * width), BF16), shape((depth, 2 * kv_width), BF16)]
        + [shape((cap, rows), BF16)],
        [HBM] * 7,
        [VMEM] * (pairs + 5),
        [
            pltpu.SMEM((cap,), jnp.int32),
            pltpu.SMEM((ctx,), jnp.int32),
            pltpu.VMEM((rows, 2 * half * (pairs + 2)), BF16),
            pltpu.SemaphoreType.DMA((pairs + 2,)),
            pltpu.SemaphoreType.DMA((6,)),
        ],
        cost(2 * cap * rows * model // 2, rows * model),
        "pick",
    )(select_index, valid_count, tokens, queries, out_grad, key_matrix, value_matrix)
    got = [
        move(picked[i], lambda a, b, t, i=i: (a ^ (2 * i + 1 + t % 2), b, t)) for i in range(pairs)
    ] + [a_swap(picked[pairs], size - 1)]
    other = t_swap(jnp.concatenate(got, axis=1), 1)
    qds = [qd] + [a_swap(qd, s) for s in range(1, size)]

    part, *cols = call(
        functools.partial(project_body, size, inner, half),
        [shape((slots, 2 * kv_width), BF16)]
        + [shape((slots, depth), BF16)] * inner
        + [shape((depth, 2 * kv_width), BF16)] * (inner - 1),
        [VMEM] * (pairs + 2 * inner + 2),
        [VMEM] * (2 * inner),
        [pltpu.VMEM((slots, 2 * half), BF16)],
        cost(4 * slots * half * 2 * kv_width, 4 * half * (slots + 2 * kv_width)),
        "project",
    )(*got, other, own, weights, *kv_swapped)
    cols, w_own = cols[:inner], [weights] + cols[inner:]
    parts = [part] + [a_swap(part, s) for s in range(1, size)]
    cols = cols[:1] + [b_swap(after(x, parts[1]), s + 1) for s, x in enumerate(cols[1:])]
    while len(parts) > 1:
        parts = [x.astype(F32) + y.astype(F32) for x, y in zip(parts[::2], parts[1::2])]
    kv = parts[0].astype(BF16)
    kvs = [kv] + [b_swap(kv, s) for s in range(1, inner)]

    block = shape((slots, 2 * kv_width), BF16)
    attended, query_gradient, kept, *sent = call(
        functools.partial(attend_body, size, inner, cap, group),
        [shape((cap, width), BF16)] * 2
        + [shape((slots, 2 * kv_width), F32)]
        + [block] * (inner - 1),
        [SMEM] + [VMEM] * (size + inner),
        [VMEM] * (2 + inner),
        [pltpu.VMEM((slots * group, HEAD), BF16)] * 2,
        cost(12 * slots * group * slots * inner * HEAD, 4 * slots * width),
        "attend",
    )(valid_count, *qds, *kvs)

    terms = [kept] + [b_swap(x, s + 1) for s, x in enumerate(sent)]
    piece = shape((size // 2 * cap, 2 * kv_width), BF16)
    grads, low, high = call(
        functools.partial(total_pieces_body, size, inner, cap),
        [block, piece, piece],
        [VMEM] * inner,
        [VMEM] * 3,
        (),
        cost(slots * kv_width * 4, 16 * slots * kv_width),
        "grads_total",
    )(*terms)

    held, heads, step = [low], [0], size // 2
    out = [high]
    while step:
        out = out[0] if len(out) == 1 else jnp.concatenate(out, axis=0)
        back = t_swap(out, step)
        count = step * cap
        held += [back[i * count : (i + 1) * count] for i in range(len(heads))]
        heads += [h ^ step for h in heads]
        step //= 2
        out = [x[step * cap :] for x in held]
        held = [x[: step * cap] if step else x for x in held]
    head_grads = [held[heads.index(s)] for s in range(size)]

    w_heads, order, step = [w_own], [0], size // 2
    while step:
        w_heads = w_heads + [[t_swap(x, step) for x in ws] for ws in w_heads]
        order = order + [o ^ step for o in order]
        step //= 2
    w_heads = [w_heads[order.index(s)] for s in range(size)]

    row_grad = call(
        functools.partial(rows_body, size, inner),
        shape((cap, 2 * half), BF16),
        [VMEM] * (size + size * inner),
        VMEM,
        (),
        cost(4 * cap * size * 2 * kv_width * half, 8 * size * kv_width * half),
        "row_grad",
    )(*head_grads, *[x for ws in w_heads for x in ws])
    swapped = move(row_grad, lambda a, b, t: (t % 2 * (size // 2) + t // 2, b, a))

    ready = after(grads, row_grad)
    all_grads = [grads] + [b_swap(ready, s) for s in range(1, inner)]
    key_weight_grad, value_weight_grad = call(
        functools.partial(weight_body, inner),
        [shape((depth, kv_width), BF16)] * 2,
        [VMEM] * (2 * inner),
        [VMEM] * 2,
        (),
        cost(4 * slots * half * 2 * kv_width, 16 * half * kv_width),
        "weight_grads",
    )(*cols, *all_grads)

    token_grad = pl.pallas_call(
        scatter_body,
        out_shape=shape((rows, 2 * half), BF16),
        grid=(4,),
        in_specs=[
            pl.BlockSpec((cap, rows), lambda i: (0, 0)),
            pl.BlockSpec((cap, half // 2), lambda i: (0, i)),
        ],
        out_specs=pl.BlockSpec((rows, half // 2), lambda i: (0, i)),
        cost_estimate=cost(4 * rows * cap * half, 4 * rows * half),
        name="scatter",
    )(hot, swapped)
    return attended, query_gradient, token_grad, key_weight_grad, value_weight_grad


def solution(mesh):
    split = P("ctx", "tp")
    in_specs = (P("ctx", None), P("ctx"), P(), split, split, split, split)
    return jax.shard_map(
        local, mesh=mesh, in_specs=in_specs, out_specs=(split,) * 5, check_vma=False
    )
```

```python
import functools
import math

import jax
import jax.numpy as jnp
from jax import lax
from jax.experimental import pallas as pl
from jax.experimental.pallas import tpu as pltpu
from jax.sharding import PartitionSpec as P

HEAD = 128
NEG = -1e30
HIDDEN = 1 << 30
HINT = 2 * 10**10
F32 = jnp.float32
BF16 = jnp.bfloat16


VMEM = pl.BlockSpec(memory_space=pltpu.VMEM)
SMEM = pl.BlockSpec(memory_space=pltpu.SMEM)
HBM = pl.BlockSpec(memory_space=pltpu.HBM)


def dot(x, y, cx, cy):
    return lax.dot_general(x, y, (((cx,), (cy,)), ((), ())), preferred_element_type=F32)


def place(inner):
    ctx = lax.axis_index("ctx")
    return ctx // inner, lax.rem(ctx, inner), lax.axis_index("tp")


def call(body, outs, in_specs, out_specs, scratch=(), cost=None, name=None):
    return pl.pallas_call(
        body,
        out_shape=outs,
        in_specs=in_specs,
        out_specs=out_specs,
        scratch_shapes=list(scratch),
        compiler_params=pltpu.CompilerParams(vmem_limit_bytes=48 * 2**20),
        cost_estimate=cost,
        name=name,
    )


def cost(flops, nbytes):
    return pl.CostEstimate(flops=int(flops), bytes_accessed=int(nbytes), transcendentals=0)


def one_hot(select_ref, limit, rows, width):
    at = lax.broadcasted_iota(jnp.int32, (rows, width), 0)
    wanted = jnp.full((rows, width), -1, jnp.int32)
    for j in range(rows):
        wanted = jnp.where((at == j) & (j < limit), select_ref[j], wanted)
    column = lax.broadcasted_iota(jnp.int32, (rows, width), 1)
    return jnp.where(column == wanted, 1.0, 0.0).astype(BF16)


def pick_body(
    size, inner, half, select_hbm, count_hbm, tokens_ref, q_ref, og_ref, k_ref, v_ref, *rest
):
    pairs = size // 2 - 1
    outs, (qd_ref, w_ref, hot_ref) = rest[: pairs + 2], rest[pairs + 2 : pairs + 5]
    select_ref, count_ref, buf, sems, side = rest[pairs + 5 :]
    a, b, t = place(inner)
    cap, rows = outs[0].shape[0], tokens_ref.shape[0]
    width = q_ref.shape[1]
    core = lax.rem(t, 2)
    first = [
        pltpu.make_async_copy(select_hbm, select_ref, side.at[0]),
        pltpu.make_async_copy(count_hbm, count_ref, side.at[1]),
    ]
    for c in first:
        c.start()
    starts = [(a ^ (2 * i + 1 + core)) * (2 * half) for i in range(pairs)]
    starts += [(a ^ (size - 1)) * (2 * half) + core * half, a * (2 * half)]
    copies = []
    for i, at in enumerate(starts):
        wide = outs[i].shape[1]
        copies.append(
            pltpu.make_async_copy(
                tokens_ref.at[:, pl.ds(pl.multiple_of(at, 128), wide)],
                buf.at[:, 2 * half * i : 2 * half * i + wide],
                sems.at[i],
            )
        )
        copies[i].start()
    others = [
        pltpu.make_async_copy(q_ref, qd_ref.at[:, :width], side.at[2]),
        pltpu.make_async_copy(og_ref, qd_ref.at[:, width:], side.at[3]),
        pltpu.make_async_copy(k_ref, w_ref.at[:, : k_ref.shape[1]], side.at[4]),
        pltpu.make_async_copy(v_ref, w_ref.at[:, k_ref.shape[1] :], side.at[5]),
    ]
    for c in others:
        c.start()
    for c in first:
        c.wait()
    hot = one_hot(select_ref, cap, cap, rows)
    slot = lax.broadcasted_iota(jnp.int32, (cap, rows), 0)
    live = slot < count_ref[a * inner + b]
    hot_ref[...] = jnp.where(live, hot.astype(F32), 0.0).astype(BF16)
    for i in range(len(starts)):
        copies[i].wait()
        wide = outs[i].shape[1]
        outs[i][...] = dot(hot, buf[:, 2 * half * i : 2 * half * i + wide], 1, 0).astype(BF16)
    for c in others:
        c.wait()


def project_body(size, inner, half, *refs):
    pairs = size // 2 - 1
    got, other_ref, own_ref = refs[: pairs + 1], refs[pairs + 1], refs[pairs + 2]
    w_refs, outs = refs[pairs + 3 : pairs + 3 + inner], refs[pairs + 3 + inner :]
    part_ref, cols, rows_ref = outs[0], outs[1 : inner + 1], outs[-1]
    a, b, t = place(inner)
    cap = own_ref.shape[0]
    core = lax.rem(t, 2)

    def to(z):
        return pl.ds(pl.multiple_of(z * cap, cap), cap)

    def side(k):
        return pl.ds(pl.multiple_of(k * half, 128), half)

    rows_ref[to(a), :] = own_ref[...]
    for i in range(pairs):
        rows_ref[to(a ^ (2 * i + 1 + core)), :] = got[i][...]
        rows_ref[to(a ^ (2 * i + 2 - core)), :] = other_ref[:, 2 * half * i : 2 * half * (i + 1)]
    rows_ref[to(a ^ (size - 1)), side(core)] = got[pairs][...]
    rows_ref[to(a ^ (size - 1)), side(1 - core)] = other_ref[:, 2 * half * pairs :]
    depth = w_refs[0].shape[0]
    total = None
    for s in range(inner):
        part = rows_ref[:, pl.ds(pl.multiple_of((b ^ s) * depth, 128), depth)]
        cols[s][...] = part
        term = dot(part, w_refs[s][...], 1, 0)
        total = term if total is None else total + term
    part_ref[...] = total.astype(BF16)


def attend_body(size, inner, cap, group, count_ref, *refs):
    qds, kvs = refs[:size], refs[size : size + inner]
    att_ref, dq_ref, kept_ref, sent_ref, q_all, do_all = refs[size + inner :]
    a, b, t = place(inner)
    width = group * HEAD
    block = group * cap
    scale = 1.0 / math.sqrt(HEAD)
    slot = lax.broadcasted_iota(jnp.int32, (cap, HEAD), 0)
    far, far_other = qds[2][...], qds[3][...]
    swapped = jnp.concatenate([far_other[cap:], far_other[:cap]], axis=0)
    odd = lax.rem(a, 2) == 1
    far_q, far_do = jnp.where(odd, swapped, far), jnp.where(odd, far, swapped)
    for s in range(size):
        count = count_ref[(a ^ s) * inner + b]
        if s < 2:
            q_rows, do_rows = qds[s][:, :width], qds[s][:, width:]
        else:
            far_rows = slice((s - 2) * cap, (s - 1) * cap)
            q_rows, do_rows = far_q[far_rows], far_do[far_rows]
        for g in range(group):
            to = slice(s * block + g * cap, s * block + (g + 1) * cap)
            q_all[to, :] = q_rows[:, g * HEAD : (g + 1) * HEAD]
            rows = do_rows[:, g * HEAD : (g + 1) * HEAD]
            do_all[to, :] = jnp.where(slot < count, rows.astype(F32), 0.0).astype(BF16)
    kv = jnp.concatenate([r[...] for r in kvs], axis=0)
    keys, values = kv[:, :HEAD], kv[:, HEAD:]
    keys_t = keys.astype(F32).T.astype(BF16)
    values_t = values.astype(F32).T.astype(BF16)
    row = lax.broadcasted_iota(jnp.int32, (cap, block), 0)
    pieces = []
    for s in range(inner):
        for z in range(size):
            shard = z * inner + (b ^ s)
            pieces.append(jnp.where(row < count_ref[shard], shard * cap + row, HIDDEN))
    key_at = jnp.concatenate(pieces, axis=0)
    column = lax.rem(lax.broadcasted_iota(jnp.int32, (1, block), 1), cap)
    dk = dv = None
    for s in range(size):
        shard = (a ^ s) * inner + b
        live = column < count_ref[shard]
        q = q_all[s * block : (s + 1) * block, :]
        do = do_all[s * block : (s + 1) * block, :]
        scores = dot(keys, q, 1, 1) * scale
        scores = jnp.where(key_at <= shard * cap + column, scores, NEG)
        terms = jnp.exp(scores - jnp.max(scores, axis=0, keepdims=True))
        probs = terms * (1.0 / jnp.sum(terms, axis=0, keepdims=True))
        weights = probs.astype(BF16)
        att = jnp.where(live, dot(values_t, weights, 1, 0), 0.0).astype(BF16).astype(F32)
        do_t = do.astype(F32).T
        out_dot = jnp.sum(do_t * att, axis=0, keepdims=True)
        grad_probs = dot(values, do, 1, 1)
        grad_scores = (probs * (grad_probs - out_dot) * scale).astype(BF16)
        k_term, v_term = dot(grad_scores, q, 1, 0), dot(weights, do, 1, 0)
        dk = k_term if dk is None else dk + k_term
        dv = v_term if dv is None else dv + v_term
        if s == 0:
            att_rows = att.T.astype(BF16)
            dq_rows = dot(keys_t, grad_scores, 1, 0).T.astype(BF16)
            for g in range(group):
                att_ref[:, g * HEAD : (g + 1) * HEAD] = att_rows[g * cap : (g + 1) * cap, :]
                dq_ref[:, g * HEAD : (g + 1) * HEAD] = dq_rows[g * cap : (g + 1) * cap, :]
    for ref in (kept_ref, sent_ref):
        ref[:, :HEAD] = dk.astype(ref.dtype)
        ref[:, HEAD:] = dv.astype(ref.dtype)


def total_body(size, inner, cap, *refs):
    terms, (grads_ref, keep_ref, send_ref) = refs[:inner], refs[inner:]
    slots = size * cap
    for s in range(inner):
        total = None
        for j in range(inner):
            term = terms[j][(s ^ j) * slots : ((s ^ j) + 1) * slots, :].astype(F32)
            total = term if total is None else total + term
        grads_ref[s * slots : (s + 1) * slots, :] = total.astype(BF16)
    rows = slots // 2
    core = lax.rem(lax.axis_index("tp"), 2)
    keep_ref[...] = grads_ref[pl.ds(pl.multiple_of(core * rows, rows), rows), :]
    send_ref[...] = grads_ref[pl.ds(pl.multiple_of((1 - core) * rows, rows), rows), :]


def weight_body(inner, *refs):
    cols, (grads_ref, k_ref, v_ref) = refs[:inner], refs[inner:]
    slots = cols[0].shape[0]
    total = None
    for s in range(inner):
        term = dot(cols[s][...], grads_ref[s * slots : (s + 1) * slots, :], 0, 0)
        total = term if total is None else total + term
    width = k_ref.shape[1]
    k_ref[...] = total[:, :width].astype(BF16)
    v_ref[...] = total[:, width:].astype(BF16)


def rows_body(size, inner, cap, *refs):
    own, pair, weights, outs = refs[0], refs[1], refs[2 : 2 + 2 * inner], refs[2 + 2 * inner :]
    outs, total_ref = outs[:-1], outs[-1]
    a, b, t = place(inner)
    depth = weights[0].shape[0]
    for j in range(inner):
        total = dot(own[...], weights[j][...], 1, 1) + dot(pair[...], weights[inner + j][...], 1, 1)
        total_ref[:, pl.ds(pl.multiple_of((b ^ j) * depth, 128), depth)] = total.astype(BF16)
    for m in range(len(outs)):
        at = (t // 2) ^ m
        outs[m][...] = total_ref[pl.ds(pl.multiple_of(at * cap, cap), cap), :]


def scatter_body(parts, hot_ref, *refs):
    rows_refs, out_ref, buf, sems = refs[:parts], refs[parts], refs[parts + 1], refs[parts + 2]
    count = sems.shape[0]
    wide = out_ref.shape[1] // count
    hot = hot_ref[...]
    copies = []
    for i in range(count):
        cols = slice(i * wide, (i + 1) * wide)
        total = None
        for r in rows_refs:
            term = dot(hot, r[:, cols], 0, 0)
            total = term if total is None else total + term
        buf[:, cols] = total.astype(BF16)
        copies.append(pltpu.make_async_copy(buf.at[:, cols], out_ref.at[:, cols], sems.at[i]))
        copies[i].start()
    for c in copies:
        c.wait()


def after(x, *others):
    return lax.optimization_barrier((x, *others))[0]


def local(tokens, select_index, valid_count, queries, key_matrix, value_matrix, out_grad):
    size, ctx = lax.axis_size("tp"), lax.axis_size("ctx")
    inner = ctx // size
    cap = select_index.shape[0]
    rows, model = tokens.shape
    depth, kv_width = key_matrix.shape
    width = queries.shape[1]
    group = width // kv_width
    half = inner * depth // 2
    slots = size * cap
    pairs = size // 2 - 1
    shape = jax.ShapeDtypeStruct

    def a_swap(x, s):
        return lax.ppermute(x, "ctx", [(j, (j // inner ^ s) * inner + j % inner) for j in range(ctx)])

    def b_swap(x, s):
        return lax.ppermute(x, "ctx", [(j, j // inner * inner + (j % inner ^ s)) for j in range(ctx)])

    def t_swap(x, s):
        return lax.ppermute(x, "tp", [(j, j ^ s) for j in range(size)])

    def move(x, target):
        index = [(a, b, t) for a in range(size) for b in range(inner) for t in range(size)]
        flat = lambda a, b, t: (a * inner + b) * size + t
        return lax.ppermute(x, ("ctx", "tp"), [(flat(*i), flat(*target(*i))) for i in index])

    inputs = (select_index, valid_count, tokens, queries, out_grad, key_matrix, value_matrix)
    *picked, own, qd, weights, hot = call(
        functools.partial(pick_body, size, inner, half),
        [shape((cap, 2 * half), BF16)] * pairs
        + [shape((cap, half), BF16), shape((cap, 2 * half), BF16)]
        + [shape((cap, 2 * width), BF16), shape((depth, 2 * kv_width), BF16)]
        + [shape((cap, rows), BF16)],
        [HBM] * 7,
        [VMEM] * (pairs + 5),
        [
            pltpu.SMEM((cap,), jnp.int32),
            pltpu.SMEM((ctx,), jnp.int32),
            pltpu.VMEM((rows, 2 * half * (pairs + 2)), BF16),
            pltpu.SemaphoreType.DMA((pairs + 2,)),
            pltpu.SemaphoreType.DMA((6,)),
        ],
        cost(HINT, rows * model),
        "pick",
    )(*[pltpu.with_memory_space_constraint(x, pltpu.HBM) for x in inputs])
    got = [
        move(picked[i], lambda a, b, t, i=i: (a ^ (2 * i + 1 + t % 2), b, t)) for i in range(pairs)
    ] + [a_swap(picked[pairs], size - 1)]
    k_far = [b_swap(key_matrix, s) for s in range(1, inner)]
    v_far = [b_swap(value_matrix, s) for s in range(1, inner)]
    w_own = [weights] + [jnp.concatenate(x, axis=1) for x in zip(k_far, v_far)]
    k_pair = [t_swap(x, 1) for x in k_far]
    other = t_swap(jnp.concatenate(got, axis=1), 1)
    near = a_swap(qd, 1)
    both = jnp.concatenate([qd, near], axis=0)
    odd = lax.rem(lax.axis_index("ctx") // inner, 2) == 1
    far = a_swap(jnp.where(odd, both[:, width:], both[:, :width]), 2)
    far_other = a_swap(far, 1)
    qds = [qd, near, far, far_other]

    part, *cols = call(
        functools.partial(project_body, size, inner, half),
        [shape((slots, 2 * kv_width), BF16)]
        + [shape((slots, depth), BF16)] * inner,
        [VMEM] * (pairs + inner + 3),
        [VMEM] * (inner + 1),
        [pltpu.VMEM((slots, 2 * half), BF16)],
        cost(HINT, 4 * half * (slots + 2 * kv_width)),
        "project",
    )(*got, other, own, *w_own)
    parts = [part] + [a_swap(part, s) for s in range(1, size)]
    first = parts[1]
    cols = cols[:1] + [b_swap(after(x, first), s + 1) for s, x in enumerate(cols[1:])]
    while len(parts) > 1:
        parts = [x.astype(F32) + y.astype(F32) for x, y in zip(parts[::2], parts[1::2])]
    kv = parts[0].astype(BF16)
    kvs = [kv] + [b_swap(kv, s) for s in range(1, inner)]

    terms = (slots * inner, 2 * kv_width)
    attended, query_gradient, kept, sent = call(
        functools.partial(attend_body, size, inner, cap, group),
        [shape((cap, width), BF16)] * 2 + [shape(terms, F32), shape(terms, BF16)],
        [SMEM] + [VMEM] * (size + inner),
        [VMEM] * 4,
        [pltpu.VMEM((slots * group, HEAD), BF16)] * 2,
        cost(12 * slots * group * slots * inner * HEAD, 4 * slots * width),
        "attend",
    )(valid_count, *qds, after(kvs[0], cols[1]), *kvs[1:])

    piece = shape((size // 2 * cap, 2 * kv_width), BF16)
    grads, keep, send = call(
        functools.partial(total_body, size, inner, cap),
        [shape(terms, BF16), piece, piece],
        [VMEM] * inner,
        [VMEM] * 3,
        (),
        cost(slots * inner * kv_width * 4, 16 * slots * inner * kv_width),
        "grads_total",
    )(kept, *[b_swap(sent, s) for s in range(1, inner)])
    pair_grads = t_swap(send, 1)
    w_pair = [t_swap(after(weights, first), 1)] + [
        jnp.concatenate([k, t_swap(after(v, first), 1)], axis=1) for k, v in zip(k_pair, v_far)
    ]

    row_grads = call(
        functools.partial(rows_body, size, inner, cap),
        [shape((cap, 2 * half), BF16)] * (size // 2),
        [VMEM] * (2 + 2 * inner),
        [VMEM] * (size // 2),
        [pltpu.VMEM((size // 2 * cap, 2 * half), BF16)],
        cost(4 * cap * size * 2 * kv_width * half, 8 * size * kv_width * half),
        "row_grad",
    )(keep, pair_grads, *w_own, *w_pair)
    swapped = [
        move(x, lambda a, b, t, m=m: (t % 2 * (size // 2) + (t // 2 ^ m), b, a))
        for m, x in enumerate(row_grads)
    ]
    key_weight_grad, value_weight_grad = call(
        functools.partial(weight_body, inner),
        [shape((depth, kv_width), BF16)] * 2,
        [VMEM] * (inner + 1),
        [VMEM] * 2,
        (),
        cost(4 * slots * half * 2 * kv_width, 16 * half * kv_width),
        "weight_grads",
    )(*cols, after(grads, row_grads[0]))

    chunks = 4
    token_grad = call(
        functools.partial(scatter_body, size // 2),
        shape((rows, 2 * half), BF16),
        [VMEM] * (1 + size // 2),
        HBM,
        [pltpu.VMEM((rows, 2 * half), BF16), pltpu.SemaphoreType.DMA((chunks,))],
        cost(4 * rows * cap * half, 4 * rows * half),
        "scatter",
    )(hot, *swapped)
    return attended, query_gradient, token_grad, key_weight_grad, value_weight_grad


def solution(mesh):
    split = P("ctx", "tp")
    in_specs = (P("ctx", None), P("ctx"), P(), split, split, split, split)
    return jax.shard_map(
        local, mesh=mesh, in_specs=in_specs, out_specs=(split,) * 5, check_vma=False
    )
```

```python
import functools
import math

import jax
import jax.numpy as jnp
from jax import lax
from jax.experimental import pallas as pl
from jax.experimental.pallas import tpu as pltpu
from jax.sharding import PartitionSpec as P

HEAD = 128
NEG = -1e30
HIDDEN = 1 << 30
HINT = 2 * 10**10
F32 = jnp.float32
BF16 = jnp.bfloat16


VMEM = pl.BlockSpec(memory_space=pltpu.VMEM)
SMEM = pl.BlockSpec(memory_space=pltpu.SMEM)
HBM = pl.BlockSpec(memory_space=pltpu.HBM)


def dot(x, y, cx, cy):
    return lax.dot_general(x, y, (((cx,), (cy,)), ((), ())), preferred_element_type=F32)


def place(inner):
    ctx = lax.axis_index("ctx")
    return ctx // inner, lax.rem(ctx, inner), lax.axis_index("tp")


def call(body, outs, in_specs, out_specs, scratch=(), cost=None, name=None):
    return pl.pallas_call(
        body,
        out_shape=outs,
        in_specs=in_specs,
        out_specs=out_specs,
        scratch_shapes=list(scratch),
        compiler_params=pltpu.CompilerParams(vmem_limit_bytes=48 * 2**20),
        cost_estimate=cost,
        name=name,
    )


def cost(flops, nbytes):
    return pl.CostEstimate(flops=int(flops), bytes_accessed=int(nbytes), transcendentals=0)


def one_hot(select_ref, limit, rows, width):
    at = lax.broadcasted_iota(jnp.int32, (rows, width), 0)
    wanted = jnp.full((rows, width), -1, jnp.int32)
    for j in range(rows):
        wanted = jnp.where((at == j) & (j < limit), select_ref[j], wanted)
    column = lax.broadcasted_iota(jnp.int32, (rows, width), 1)
    return jnp.where(column == wanted, 1.0, 0.0).astype(BF16)


def pick_body(
    size, inner, half, select_hbm, count_hbm, tokens_ref, q_ref, og_ref, k_ref, v_ref, *rest
):
    pairs = size // 2 - 1
    outs, (qd_ref, w_ref, hot_ref, live_ref, order_ref) = rest[: pairs + 2], rest[pairs + 2 : pairs + 7]
    select_ref, count_ref, buf, og_buf, sems, side = rest[pairs + 7 :]
    a, b, t = place(inner)
    cap, rows = outs[0].shape[0], tokens_ref.shape[0]
    width = q_ref.shape[1]
    core = lax.rem(t, 2)
    first = [
        pltpu.make_async_copy(select_hbm, select_ref, side.at[0]),
        pltpu.make_async_copy(count_hbm, count_ref, side.at[1]),
    ]
    for c in first:
        c.start()
    starts = [(a ^ (2 * i + 1 + core)) * (2 * half) for i in range(pairs)]
    starts += [(a ^ (size - 1)) * (2 * half) + core * half, a * (2 * half)]
    copies = []
    for i, at in enumerate(starts):
        wide = outs[i].shape[1]
        copies.append(
            pltpu.make_async_copy(
                tokens_ref.at[:, pl.ds(pl.multiple_of(at, 128), wide)],
                buf.at[:, 2 * half * i : 2 * half * i + wide],
                sems.at[i],
            )
        )
        copies[i].start()
    others = [
        pltpu.make_async_copy(q_ref, qd_ref.at[:, :width], side.at[2]),
        pltpu.make_async_copy(og_ref, og_buf, side.at[3]),
        pltpu.make_async_copy(k_ref, w_ref.at[:, : k_ref.shape[1]], side.at[4]),
        pltpu.make_async_copy(v_ref, w_ref.at[:, k_ref.shape[1] :], side.at[5]),
    ]
    for c in others:
        c.start()
    for c in first:
        c.wait()
    hot = one_hot(select_ref, cap, cap, rows)
    slot = lax.broadcasted_iota(jnp.int32, (cap, rows), 0)
    live = slot < count_ref[a * inner + b]
    hot_ref[...] = jnp.where(live, hot.astype(F32), 0.0).astype(BF16)
    for i in range(len(starts)):
        copies[i].wait()
        wide = outs[i].shape[1]
        outs[i][...] = dot(hot, buf[:, 2 * half * i : 2 * half * i + wide], 1, 0).astype(BF16)
    row = lax.broadcasted_iota(jnp.int32, (cap, HEAD), 0)
    live_ref[...] = jnp.where(row < count_ref[a * inner + b], 1.0, 0.0)
    for s in range(inner):
        for z in range(size):
            shard = z * inner + (b ^ s)
            at = jnp.where(row < count_ref[shard], shard * cap + row, HIDDEN)
            order_ref[(s * size + z) * cap : (s * size + z + 1) * cap, :] = at
    for c in others:
        c.wait()
    qd_ref[:, width:] = og_buf[...] * live_ref[:, :1].astype(BF16)


def project_body(size, inner, half, *refs):
    pairs = size // 2 - 1
    got, other_ref, own_ref = refs[: pairs + 1], refs[pairs + 1], refs[pairs + 2]
    w_refs, outs = refs[pairs + 3 : pairs + 3 + inner], refs[pairs + 3 + inner :]
    part_ref, cols, rows_ref = outs[0], outs[1 : inner + 1], outs[-1]
    a, b, t = place(inner)
    cap = own_ref.shape[0]
    core = lax.rem(t, 2)

    def to(z):
        return pl.ds(pl.multiple_of(z * cap, cap), cap)

    def side(k):
        return pl.ds(pl.multiple_of(k * half, 128), half)

    rows_ref[to(a), :] = own_ref[...]
    for i in range(pairs):
        rows_ref[to(a ^ (2 * i + 1 + core)), :] = got[i][...]
        rows_ref[to(a ^ (2 * i + 2 - core)), :] = other_ref[:, 2 * half * i : 2 * half * (i + 1)]
    rows_ref[to(a ^ (size - 1)), side(core)] = got[pairs][...]
    rows_ref[to(a ^ (size - 1)), side(1 - core)] = other_ref[:, 2 * half * pairs :]
    depth = w_refs[0].shape[0]
    total = None
    for s in range(inner):
        part = rows_ref[:, pl.ds(pl.multiple_of((b ^ s) * depth, 128), depth)]
        cols[s][...] = part
        term = dot(part, w_refs[s][...], 1, 0)
        total = term if total is None else total + term
    part_ref[...] = total.astype(BF16)


def attend_body(size, inner, cap, group, live_ref, order_ref, *refs):
    qds, kvs = refs[:size], refs[size : size + inner]
    att_ref, dq_ref, kept_ref, sent_ref, q_all, do_all = refs[size + inner :]
    a, b, t = place(inner)
    width = group * HEAD
    block = group * cap
    scale = 1.0 / math.sqrt(HEAD)
    far, far_other = qds[2][...], qds[3][...]
    swapped = jnp.concatenate([far_other[cap:], far_other[:cap]], axis=0)
    odd = lax.rem(a, 2) == 1
    far_q, far_do = jnp.where(odd, swapped, far), jnp.where(odd, far, swapped)
    for s in range(size):
        if s < 2:
            q_rows, do_rows = qds[s][:, :width], qds[s][:, width:]
        else:
            far_rows = slice((s - 2) * cap, (s - 1) * cap)
            q_rows, do_rows = far_q[far_rows], far_do[far_rows]
        for g in range(group):
            to = slice(s * block + g * cap, s * block + (g + 1) * cap)
            q_all[to, :] = q_rows[:, g * HEAD : (g + 1) * HEAD]
            do_all[to, :] = do_rows[:, g * HEAD : (g + 1) * HEAD]
    kv = jnp.concatenate([r[...] for r in kvs], axis=0)
    keys, values = kv[:, :HEAD], kv[:, HEAD:]
    keys_t = keys.astype(F32).T.astype(BF16)
    values_t = values.astype(F32).T.astype(BF16)
    key_at = order_ref[:, :1]
    step = size if kv.shape[0] <= 512 else 1
    dk = dv = None
    for s in range(0, size, step):
        cols = slice(s * block, (s + step) * block)
        column = lax.broadcasted_iota(jnp.int32, (1, step * block), 1)
        shard = ((a ^ (s + column // block)) * inner) + b
        query_at = shard * cap + lax.rem(column, cap)
        q, do = q_all[cols, :], do_all[cols, :]
        scores = dot(keys, q, 1, 1) * scale
        scores = jnp.where(key_at <= query_at, scores, NEG)
        terms = jnp.exp(scores - jnp.max(scores, axis=0, keepdims=True))
        probs = terms * (1.0 / jnp.sum(terms, axis=0, keepdims=True))
        weights = probs.astype(BF16)
        att = dot(values_t, weights, 1, 0).astype(BF16).astype(F32)
        out_dot = jnp.sum(do.astype(F32).T * att, axis=0, keepdims=True)
        grad_probs = dot(values, do, 1, 1)
        grad_scores = (probs * (grad_probs - out_dot) * scale).astype(BF16)
        k_term, v_term = dot(grad_scores, q, 1, 0), dot(weights, do, 1, 0)
        dk = k_term if dk is None else dk + k_term
        dv = v_term if dv is None else dv + v_term
        if s == 0:
            att_rows = att[:, :block].T
            dq_rows = dot(keys_t, grad_scores[:, :block], 1, 0).T.astype(BF16)
            for g in range(group):
                rows, to = slice(g * cap, (g + 1) * cap), slice(g * HEAD, (g + 1) * HEAD)
                att_ref[:, to] = (att_rows[rows, :] * live_ref[...]).astype(BF16)
                dq_ref[:, to] = dq_rows[rows, :]
    for ref in (kept_ref, sent_ref):
        ref[:, :HEAD] = dk.astype(ref.dtype)
        ref[:, HEAD:] = dv.astype(ref.dtype)


def total_body(size, inner, cap, *refs):
    terms, weights, (grads_ref, keep_ref, send_ref) = refs[:inner], refs[inner : 2 * inner], refs[2 * inner :]
    slots = size * cap
    for s in range(inner):
        total = None
        for j in range(inner):
            term = terms[j][(s ^ j) * slots : ((s ^ j) + 1) * slots, :].astype(F32)
            total = term if total is None else total + term
        grads_ref[s * slots : (s + 1) * slots, :] = total.astype(BF16)
    a, b, t = place(inner)
    rows = slots // 2
    core = lax.rem(t, 2)
    depth = weights[0].shape[0]
    for ref, side in ((send_ref, 1 - core), (keep_ref, core)):
        part = grads_ref[pl.ds(pl.multiple_of(side * rows, rows), rows), :]
        for j in range(inner):
            term = dot(part, weights[j][...], 1, 1)
            ref[:, pl.ds(pl.multiple_of((b ^ j) * depth, 128), depth)] = term.astype(ref.dtype)


def weight_body(inner, *refs):
    cols, (grads_ref, att_ref, dq_ref, k_ref, v_ref, att_out, dq_out) = refs[:inner], refs[inner:]
    att_out[...] = att_ref[...]
    dq_out[...] = dq_ref[...]
    slots = cols[0].shape[0]
    total = None
    for s in range(inner):
        term = dot(cols[s][...], grads_ref[s * slots : (s + 1) * slots, :], 0, 0)
        total = term if total is None else total + term
    width = k_ref.shape[1]
    k_ref[...] = total[:, :width].astype(BF16)
    v_ref[...] = total[:, width:].astype(BF16)


def pair_body(cap, keep_ref, got_ref, *outs):
    t = lax.axis_index("tp")
    for m in range(len(outs)):
        at = pl.ds(pl.multiple_of(((t // 2) ^ m) * cap, cap), cap)
        outs[m][...] = (keep_ref[at, :] + got_ref[at, :].astype(F32)).astype(BF16)


def scatter_body(parts, hot_ref, *refs):
    rows_refs, out_ref, buf, sems = refs[:parts], refs[parts], refs[parts + 1], refs[parts + 2]
    count = sems.shape[0]
    wide = out_ref.shape[1] // count
    hot = hot_ref[...]
    copies = []
    for i in range(count):
        cols = slice(i * wide, (i + 1) * wide)
        total = None
        for r in rows_refs:
            term = dot(hot, r[:, cols], 0, 0)
            total = term if total is None else total + term
        buf[:, cols] = total.astype(BF16)
        copies.append(pltpu.make_async_copy(buf.at[:, cols], out_ref.at[:, cols], sems.at[i]))
        copies[i].start()
    for c in copies:
        c.wait()


def after(x, *others):
    return lax.optimization_barrier((x, *others))[0]


def local(tokens, select_index, valid_count, queries, key_matrix, value_matrix, out_grad):
    size, ctx = lax.axis_size("tp"), lax.axis_size("ctx")
    inner = ctx // size
    cap = select_index.shape[0]
    rows, model = tokens.shape
    depth, kv_width = key_matrix.shape
    width = queries.shape[1]
    group = width // kv_width
    half = inner * depth // 2
    slots = size * cap
    pairs = size // 2 - 1
    shape = jax.ShapeDtypeStruct

    def a_swap(x, s):
        return lax.ppermute(x, "ctx", [(j, (j // inner ^ s) * inner + j % inner) for j in range(ctx)])

    def b_swap(x, s):
        return lax.ppermute(x, "ctx", [(j, j // inner * inner + (j % inner ^ s)) for j in range(ctx)])

    def t_swap(x, s):
        return lax.ppermute(x, "tp", [(j, j ^ s) for j in range(size)])

    def move(x, target):
        index = [(a, b, t) for a in range(size) for b in range(inner) for t in range(size)]
        flat = lambda a, b, t: (a * inner + b) * size + t
        return lax.ppermute(x, ("ctx", "tp"), [(flat(*i), flat(*target(*i))) for i in index])

    inputs = (select_index, valid_count, tokens, queries, out_grad, key_matrix, value_matrix)
    *picked, own, qd, weights, hot, live, order = call(
        functools.partial(pick_body, size, inner, half),
        [shape((cap, 2 * half), BF16)] * pairs
        + [shape((cap, half), BF16), shape((cap, 2 * half), BF16)]
        + [shape((cap, 2 * width), BF16), shape((depth, 2 * kv_width), BF16)]
        + [shape((cap, rows), BF16), shape((cap, HEAD), F32)]
        + [shape((slots * inner, HEAD), jnp.int32)],
        [HBM] * 7,
        [VMEM] * (pairs + 7),
        [
            pltpu.SMEM((cap,), jnp.int32),
            pltpu.SMEM((ctx,), jnp.int32),
            pltpu.VMEM((rows, 2 * half * (pairs + 2)), BF16),
            pltpu.VMEM((cap, width), BF16),
            pltpu.SemaphoreType.DMA((pairs + 2,)),
            pltpu.SemaphoreType.DMA((6,)),
        ],
        cost(HINT, rows * model),
        "pick",
    )(*[pltpu.with_memory_space_constraint(x, pltpu.HBM) for x in inputs])
    got = [
        move(picked[i], lambda a, b, t, i=i: (a ^ (2 * i + 1 + t % 2), b, t)) for i in range(pairs)
    ] + [a_swap(picked[pairs], size - 1)]
    w_far = [[b_swap(x, s) for x in (key_matrix, value_matrix)] for s in range(1, inner)]
    w_own = [weights] + [jnp.concatenate(x, axis=1) for x in w_far]
    other = t_swap(jnp.concatenate(got, axis=1), 1)
    near = a_swap(qd, 1)
    both = jnp.concatenate([qd, near], axis=0)
    odd = lax.rem(lax.axis_index("ctx") // inner, 2) == 1
    far = a_swap(jnp.where(odd, both[:, width:], both[:, :width]), 2)

    part, *cols = call(
        functools.partial(project_body, size, inner, half),
        [shape((slots, 2 * kv_width), BF16)]
        + [shape((slots, depth), BF16)] * inner,
        [VMEM] * (pairs + inner + 3),
        [VMEM] * (inner + 1),
        [pltpu.VMEM((slots, 2 * half), BF16)],
        cost(HINT, 4 * half * (slots + 2 * kv_width)),
        "project",
    )(*got, other, own, *w_own)
    parts = [part] + [a_swap(part, s) for s in range(1, size)]
    first = parts[1]
    cols = cols[:1] + [b_swap(x, s + 1) for s, x in enumerate(cols[1:])]
    while len(parts) > 1:
        parts = [x.astype(F32) + y.astype(F32) for x, y in zip(parts[::2], parts[1::2])]
    kv = parts[0].astype(BF16)
    kvs = [kv] + [b_swap(kv, s) for s in range(1, inner)]
    far_other = a_swap(after(far, first), 1)
    qds = [qd, near, far, far_other]

    terms = (slots * inner, 2 * kv_width)
    attended, query_gradient, kept, sent = call(
        functools.partial(attend_body, size, inner, cap, group),
        [shape((cap, width), BF16)] * 2 + [shape(terms, F32), shape(terms, BF16)],
        [VMEM] * (2 + size + inner),
        [VMEM] * 4,
        [pltpu.VMEM((slots * group, HEAD), BF16)] * 2,
        cost(12 * slots * group * slots * inner * HEAD, 4 * slots * width),
        "attend",
    )(live, order, *qds, after(kvs[0], cols[1]), *kvs[1:])

    piece = (size // 2 * cap, 2 * half)
    grads, keep, send = call(
        functools.partial(total_body, size, inner, cap),
        [shape(terms, BF16), shape(piece, F32), shape(piece, BF16)],
        [VMEM] * (2 * inner),
        [VMEM] * 3,
        (),
        cost(4 * slots * half * 2 * kv_width, 8 * kv_width * half),
        "row_terms",
    )(kept, *[b_swap(sent, s) for s in range(1, inner)], *w_own)
    row_grads = call(
        functools.partial(pair_body, cap),
        [shape((cap, 2 * half), BF16)] * (size // 2),
        [VMEM] * 2,
        [VMEM] * (size // 2),
        (),
        cost(2 * slots * half, 8 * slots * half),
        "row_grad",
    )(keep, t_swap(send, 1))
    swapped = [
        move(x, lambda a, b, t, m=m: (t % 2 * (size // 2) + (t // 2 ^ m), b, a))
        for m, x in enumerate(row_grads)
    ]
    key_weight_grad, value_weight_grad, attended, query_gradient = call(
        functools.partial(weight_body, inner),
        [shape((depth, kv_width), BF16)] * 2 + [shape((cap, width), BF16)] * 2,
        [VMEM] * (inner + 3),
        [VMEM] * 4,
        (),
        cost(4 * slots * half * 2 * kv_width, 16 * half * kv_width),
        "weight_grads",
    )(*cols, after(grads, row_grads[0]), attended, query_gradient)

    chunks = 4
    token_grad = call(
        functools.partial(scatter_body, size // 2),
        shape((rows, 2 * half), BF16),
        [VMEM] * (1 + size // 2),
        HBM,
        [pltpu.VMEM((rows, 2 * half), BF16), pltpu.SemaphoreType.DMA((chunks,))],
        cost(4 * rows * cap * half, 4 * rows * half),
        "scatter",
    )(hot, *swapped)
    return attended, query_gradient, token_grad, key_weight_grad, value_weight_grad


def solution(mesh):
    split = P("ctx", "tp")
    in_specs = (P("ctx", None), P("ctx"), P(), split, split, split, split)
    return jax.shard_map(
        local, mesh=mesh, in_specs=in_specs, out_specs=(split,) * 5, check_vma=False
    )
```

```python
import functools
import math

import jax
import jax.numpy as jnp
from jax import lax
from jax.experimental import pallas as pl
from jax.experimental.pallas import tpu as pltpu
from jax.sharding import PartitionSpec as P

HEAD = 128
NEG = -1e30
HIDDEN = 1 << 30
HINT = 2 * 10**10
F32 = jnp.float32
BF16 = jnp.bfloat16


VMEM = pl.BlockSpec(memory_space=pltpu.VMEM)
SMEM = pl.BlockSpec(memory_space=pltpu.SMEM)
HBM = pl.BlockSpec(memory_space=pltpu.HBM)


def dot(x, y, cx, cy):
    return lax.dot_general(x, y, (((cx,), (cy,)), ((), ())), preferred_element_type=F32)


def place(inner):
    ctx = lax.axis_index("ctx")
    return ctx // inner, lax.rem(ctx, inner), lax.axis_index("tp")


def call(body, outs, in_specs, out_specs, scratch=(), cost=None, name=None):
    return pl.pallas_call(
        body,
        out_shape=outs,
        in_specs=in_specs,
        out_specs=out_specs,
        scratch_shapes=list(scratch),
        compiler_params=pltpu.CompilerParams(vmem_limit_bytes=48 * 2**20),
        cost_estimate=cost,
        name=name,
    )


def cost(flops, nbytes):
    return pl.CostEstimate(flops=int(flops), bytes_accessed=int(nbytes), transcendentals=0)


def one_hot(select_ref, limit, rows, width):
    at = lax.broadcasted_iota(jnp.int32, (rows, width), 0)
    wanted = jnp.full((rows, width), -1, jnp.int32)
    for j in range(rows):
        wanted = jnp.where((at == j) & (j < limit), select_ref[j], wanted)
    column = lax.broadcasted_iota(jnp.int32, (rows, width), 1)
    return jnp.where(column == wanted, 1.0, 0.0).astype(BF16)


def pick_body(
    size, inner, half, select_hbm, count_hbm, tokens_ref, k_ref, v_ref, *rest
):
    pairs = size // 2 - 1
    outs, (w_ref, hot_ref, live_ref, order_ref) = rest[: pairs + 2], rest[pairs + 2 : pairs + 6]
    select_ref, count_ref, buf, sems, side = rest[pairs + 6 :]
    a, b, t = place(inner)
    cap, rows = outs[0].shape[0], tokens_ref.shape[0]
    core = lax.rem(t, 2)
    first = [
        pltpu.make_async_copy(select_hbm, select_ref, side.at[0]),
        pltpu.make_async_copy(count_hbm, count_ref, side.at[1]),
    ]
    for c in first:
        c.start()
    starts = [(a ^ (2 * i + 1 + core)) * (2 * half) for i in range(pairs)]
    starts += [(a ^ (size - 1)) * (2 * half) + core * half, a * (2 * half)]
    copies = []
    for i, at in enumerate(starts):
        wide = outs[i].shape[1]
        copies.append(
            pltpu.make_async_copy(
                tokens_ref.at[:, pl.ds(pl.multiple_of(at, 128), wide)],
                buf.at[:, 2 * half * i : 2 * half * i + wide],
                sems.at[i],
            )
        )
        copies[i].start()
    others = [
        pltpu.make_async_copy(k_ref, w_ref.at[:, : k_ref.shape[1]], side.at[2]),
        pltpu.make_async_copy(v_ref, w_ref.at[:, k_ref.shape[1] :], side.at[3]),
    ]
    for c in others:
        c.start()
    for c in first:
        c.wait()
    hot = one_hot(select_ref, cap, cap, rows)
    slot = lax.broadcasted_iota(jnp.int32, (cap, rows), 0)
    live = slot < count_ref[a * inner + b]
    hot_ref[...] = jnp.where(live, hot.astype(F32), 0.0).astype(BF16)
    for i in range(len(starts)):
        copies[i].wait()
        wide = outs[i].shape[1]
        outs[i][...] = dot(hot, buf[:, 2 * half * i : 2 * half * i + wide], 1, 0).astype(BF16)
    row = lax.broadcasted_iota(jnp.int32, (cap, HEAD), 0)
    for s in range(size):
        count = count_ref[(a ^ s) * inner + b]
        live_ref[s * cap : (s + 1) * cap, :] = jnp.where(row < count, 1.0, 0.0).astype(BF16)
    for s in range(inner):
        for z in range(size):
            shard = z * inner + (b ^ s)
            at = jnp.where(row < count_ref[shard], shard * cap + row, HIDDEN)
            order_ref[(s * size + z) * cap : (s * size + z + 1) * cap, :] = at
    for c in others:
        c.wait()


def project_body(size, inner, half, *refs):
    pairs = size // 2 - 1
    got, other_ref, own_ref = refs[: pairs + 1], refs[pairs + 1], refs[pairs + 2]
    w_refs, outs = refs[pairs + 3 : pairs + 3 + inner], refs[pairs + 3 + inner :]
    part_ref, cols, rows_ref = outs[0], outs[1 : inner + 1], outs[-1]
    a, b, t = place(inner)
    cap = own_ref.shape[0]
    core = lax.rem(t, 2)

    def to(z):
        return pl.ds(pl.multiple_of(z * cap, cap), cap)

    def side(k):
        return pl.ds(pl.multiple_of(k * half, 128), half)

    rows_ref[to(a), :] = own_ref[...]
    for i in range(pairs):
        rows_ref[to(a ^ (2 * i + 1 + core)), :] = got[i][...]
        rows_ref[to(a ^ (2 * i + 2 - core)), :] = other_ref[:, 2 * half * i : 2 * half * (i + 1)]
    rows_ref[to(a ^ (size - 1)), side(core)] = got[pairs][...]
    rows_ref[to(a ^ (size - 1)), side(1 - core)] = other_ref[:, 2 * half * pairs :]
    depth = w_refs[0].shape[0]
    total = None
    for s in range(inner):
        part = rows_ref[:, pl.ds(pl.multiple_of((b ^ s) * depth, 128), depth)]
        cols[s][...] = part
        term = dot(part, w_refs[s][...], 1, 0)
        total = term if total is None else total + term
    part_ref[...] = total.astype(BF16)


def attend_body(size, inner, cap, group, live_ref, order_ref, *refs):
    qds, kvs = refs[:6], refs[6 : 6 + inner]
    att_ref, dq_ref, kept_ref, *sent, q_all, do_all = refs[6 + inner :]
    a, b, t = place(inner)
    width = group * HEAD
    block = group * cap
    scale = 1.0 / math.sqrt(HEAD)
    far, far_other = qds[4][...], qds[5][...]
    swapped = jnp.concatenate([far_other[cap:], far_other[:cap]], axis=0)
    odd = lax.rem(a, 2) == 1
    far_q, far_do = jnp.where(odd, swapped, far), jnp.where(odd, far, swapped)
    for s in range(size):
        if s < 2:
            q_rows, do_rows = qds[2 * s][...], qds[2 * s + 1][...]
        else:
            far_rows = slice((s - 2) * cap, (s - 1) * cap)
            q_rows, do_rows = far_q[far_rows], far_do[far_rows]
        do_rows = do_rows * live_ref[s * cap : (s + 1) * cap, :1]
        for g in range(group):
            to = slice(s * block + g * cap, s * block + (g + 1) * cap)
            q_all[to, :] = q_rows[:, g * HEAD : (g + 1) * HEAD]
            do_all[to, :] = do_rows[:, g * HEAD : (g + 1) * HEAD]
    kv = jnp.concatenate([r[...] for r in kvs], axis=0)
    keys, values = kv[:, :HEAD], kv[:, HEAD:]
    keys_t = keys.astype(F32).T.astype(BF16)
    values_t = values.astype(F32).T.astype(BF16)
    key_at = order_ref[:, :1]
    step = size if kv.shape[0] <= 512 else 1
    dk = dv = None
    for s in range(0, size, step):
        cols = slice(s * block, (s + step) * block)
        column = lax.broadcasted_iota(jnp.int32, (1, step * block), 1)
        shard = ((a ^ (s + column // block)) * inner) + b
        query_at = shard * cap + lax.rem(column, cap)
        q, do = q_all[cols, :], do_all[cols, :]
        scores = dot(keys, q, 1, 1) * scale
        scores = jnp.where(key_at <= query_at, scores, NEG)
        terms = jnp.exp(scores - jnp.max(scores, axis=0, keepdims=True))
        probs = terms * (1.0 / jnp.sum(terms, axis=0, keepdims=True))
        weights = probs.astype(BF16)
        att = dot(values_t, weights, 1, 0).astype(BF16).astype(F32)
        out_dot = jnp.sum(do.astype(F32).T * att, axis=0, keepdims=True)
        grad_probs = dot(values, do, 1, 1)
        grad_scores = (probs * (grad_probs - out_dot) * scale).astype(BF16)
        k_term, v_term = dot(grad_scores, q, 1, 0), dot(weights, do, 1, 0)
        dk = k_term if dk is None else dk + k_term
        dv = v_term if dv is None else dv + v_term
        if s == 0:
            att_rows = att[:, :block].T
            dq_rows = dot(keys_t, grad_scores[:, :block], 1, 0).T.astype(BF16)
            for g in range(group):
                rows, to = slice(g * cap, (g + 1) * cap), slice(g * HEAD, (g + 1) * HEAD)
                att_ref[:, to] = (att_rows[rows, :] * live_ref[:cap, :].astype(F32)).astype(BF16)
                dq_ref[:, to] = dq_rows[rows, :]
    rows = size * cap
    for s, ref in enumerate([kept_ref, *sent]):
        ref[:, :HEAD] = dk[s * rows : (s + 1) * rows, :].astype(ref.dtype)
        ref[:, HEAD:] = dv[s * rows : (s + 1) * rows, :].astype(ref.dtype)


def total_body(size, inner, cap, *refs):
    terms, weights, (grads_ref, keep_ref, send_ref) = refs[:inner], refs[inner : 2 * inner], refs[2 * inner :]
    slots = size * cap
    total = terms[0][...]
    for r in terms[1:]:
        total = total + r[...].astype(F32)
    grads_ref[...] = total.astype(BF16)
    a, b, t = place(inner)
    rows = slots // 2
    core = lax.rem(t, 2)
    depth = weights[0].shape[0]
    for ref, side in ((send_ref, 1 - core), (keep_ref, core)):
        part = grads_ref[pl.ds(pl.multiple_of(side * rows, rows), rows), :]
        for j in range(inner):
            term = dot(part, weights[j][...], 1, 1)
            ref[:, pl.ds(pl.multiple_of((b ^ j) * depth, 128), depth)] = term.astype(ref.dtype)


def weight_body(inner, *refs):
    cols, grads = refs[:inner], refs[inner : 2 * inner]
    att_ref, dq_ref, k_ref, v_ref, att_out, dq_out = refs[2 * inner :]
    att_out[...] = att_ref[...]
    dq_out[...] = dq_ref[...]
    total = None
    for c, g in zip(cols, grads):
        term = dot(c[...], g[...], 0, 0)
        total = term if total is None else total + term
    width = k_ref.shape[1]
    k_ref[...] = total[:, :width].astype(BF16)
    v_ref[...] = total[:, width:].astype(BF16)


def pair_body(cap, keep_ref, got_ref, *outs):
    t = lax.axis_index("tp")
    for m in range(len(outs)):
        at = pl.ds(pl.multiple_of(((t // 2) ^ m) * cap, cap), cap)
        outs[m][...] = (keep_ref[at, :] + got_ref[at, :].astype(F32)).astype(BF16)


def scatter_body(parts, hot_ref, *refs):
    rows_refs, out_ref, buf, sems = refs[:parts], refs[parts], refs[parts + 1], refs[parts + 2]
    count = sems.shape[0]
    wide = out_ref.shape[1] // count
    hot = hot_ref[...]
    copies = []
    for i in range(count):
        cols = slice(i * wide, (i + 1) * wide)
        total = None
        for r in rows_refs:
            term = dot(hot, r[:, cols], 0, 0)
            total = term if total is None else total + term
        buf[:, cols] = total.astype(BF16)
        copies.append(pltpu.make_async_copy(buf.at[:, cols], out_ref.at[:, cols], sems.at[i]))
        copies[i].start()
    for c in copies:
        c.wait()


def after(x, *others):
    return lax.optimization_barrier((x, *others))[0]


def local(tokens, select_index, valid_count, queries, key_matrix, value_matrix, out_grad):
    size, ctx = lax.axis_size("tp"), lax.axis_size("ctx")
    inner = ctx // size
    cap = select_index.shape[0]
    rows, model = tokens.shape
    depth, kv_width = key_matrix.shape
    width = queries.shape[1]
    group = width // kv_width
    half = inner * depth // 2
    slots = size * cap
    pairs = size // 2 - 1
    shape = jax.ShapeDtypeStruct

    def a_swap(x, s):
        return lax.ppermute(x, "ctx", [(j, (j // inner ^ s) * inner + j % inner) for j in range(ctx)])

    def b_swap(x, s):
        return lax.ppermute(x, "ctx", [(j, j // inner * inner + (j % inner ^ s)) for j in range(ctx)])

    def t_swap(x, s):
        return lax.ppermute(x, "tp", [(j, j ^ s) for j in range(size)])

    def move(x, target):
        index = [(a, b, t) for a in range(size) for b in range(inner) for t in range(size)]
        flat = lambda a, b, t: (a * inner + b) * size + t
        return lax.ppermute(x, ("ctx", "tp"), [(flat(*i), flat(*target(*i))) for i in index])

    inputs = (select_index, valid_count, tokens, key_matrix, value_matrix)
    *picked, own, weights, hot, live, order = call(
        functools.partial(pick_body, size, inner, half),
        [shape((cap, 2 * half), BF16)] * pairs
        + [shape((cap, half), BF16), shape((cap, 2 * half), BF16)]
        + [shape((depth, 2 * kv_width), BF16), shape((cap, rows), BF16)]
        + [shape((slots, HEAD), BF16)]
        + [shape((slots * inner, HEAD), jnp.int32)],
        [HBM] * 5,
        [VMEM] * (pairs + 6),
        [
            pltpu.SMEM((cap,), jnp.int32),
            pltpu.SMEM((ctx,), jnp.int32),
            pltpu.VMEM((rows, 2 * half * (pairs + 2)), BF16),
            pltpu.SemaphoreType.DMA((pairs + 2,)),
            pltpu.SemaphoreType.DMA((4,)),
        ],
        cost(HINT, rows * model),
        "pick",
    )(*[pltpu.with_memory_space_constraint(x, pltpu.HBM) for x in inputs])
    got = [
        move(picked[i], lambda a, b, t, i=i: (a ^ (2 * i + 1 + t % 2), b, t)) for i in range(pairs)
    ] + [a_swap(picked[pairs], size - 1)]
    w_far = [[b_swap(x, s) for x in (key_matrix, value_matrix)] for s in range(1, inner)]
    w_own = [weights] + [jnp.concatenate(x, axis=1) for x in w_far]
    other = t_swap(jnp.concatenate(got, axis=1), 1)
    near_q, near_g = a_swap(queries, 1), a_swap(out_grad, 1)
    odd = lax.rem(lax.axis_index("ctx") // inner, 2) == 1
    pair_q, pair_g = [jnp.concatenate(x, axis=0) for x in ((queries, near_q), (out_grad, near_g))]
    far = a_swap(jnp.where(odd, pair_g, pair_q), 2)

    part, *cols = call(
        functools.partial(project_body, size, inner, half),
        [shape((slots, 2 * kv_width), BF16)]
        + [shape((slots, depth), BF16)] * inner,
        [VMEM] * (pairs + inner + 3),
        [VMEM] * (inner + 1),
        [pltpu.VMEM((slots, 2 * half), BF16)],
        cost(HINT, 4 * half * (slots + 2 * kv_width)),
        "project",
    )(*got, other, own, *w_own)
    parts = [part] + [a_swap(part, s) for s in range(1, size)]
    first = parts[1]
    cols = cols[:1] + [b_swap(x, s + 1) for s, x in enumerate(cols[1:])]
    while len(parts) > 1:
        parts = [x.astype(F32) + y.astype(F32) for x, y in zip(parts[::2], parts[1::2])]
    kv = parts[0].astype(BF16)
    kvs = [kv] + [b_swap(kv, s) for s in range(1, inner)]
    far_other = a_swap(after(far, first), 1)
    qds = [queries, out_grad, near_q, near_g, far, far_other]

    terms = (slots, 2 * kv_width)
    attended, query_gradient, kept, *sent = call(
        functools.partial(attend_body, size, inner, cap, group),
        [shape((cap, width), BF16)] * 2 + [shape(terms, F32)] + [shape(terms, BF16)] * (inner - 1),
        [VMEM] * (8 + inner),
        [VMEM] * (2 + inner),
        [pltpu.VMEM((slots * group, HEAD), BF16)] * 2,
        cost(12 * slots * group * slots * inner * HEAD, 4 * slots * width),
        "attend",
    )(live, order, *qds, after(kvs[0], cols[1]), *kvs[1:])

    piece = (size // 2 * cap, 2 * half)
    grads, keep, send = call(
        functools.partial(total_body, size, inner, cap),
        [shape(terms, BF16), shape(piece, F32), shape(piece, BF16)],
        [VMEM] * (2 * inner),
        [VMEM] * 3,
        (),
        cost(4 * slots * half * 2 * kv_width, 8 * kv_width * half),
        "row_terms",
    )(kept, *[b_swap(x, s + 1) for s, x in enumerate(sent)], *w_own)
    row_grads = call(
        functools.partial(pair_body, cap),
        [shape((cap, 2 * half), BF16)] * (size // 2),
        [VMEM] * 2,
        [VMEM] * (size // 2),
        (),
        cost(2 * slots * half, 8 * slots * half),
        "row_grad",
    )(keep, t_swap(send, 1))
    swapped = [
        move(x, lambda a, b, t, m=m: (t % 2 * (size // 2) + (t // 2 ^ m), b, a))
        for m, x in enumerate(row_grads)
    ]
    far_grads = [b_swap(grads, s) for s in range(1, inner)]
    key_weight_grad, value_weight_grad, attended, query_gradient = call(
        functools.partial(weight_body, inner),
        [shape((depth, kv_width), BF16)] * 2 + [shape((cap, width), BF16)] * 2,
        [VMEM] * (2 * inner + 2),
        [VMEM] * 4,
        (),
        cost(4 * slots * half * 2 * kv_width, 16 * half * kv_width),
        "weight_grads",
    )(*cols, grads, *far_grads, after(attended, row_grads[0]), query_gradient)

    chunks = 4
    token_grad = call(
        functools.partial(scatter_body, size // 2),
        shape((rows, 2 * half), BF16),
        [VMEM] * (1 + size // 2),
        HBM,
        [pltpu.VMEM((rows, 2 * half), BF16), pltpu.SemaphoreType.DMA((chunks,))],
        cost(4 * rows * cap * half, 4 * rows * half),
        "scatter",
    )(hot, *swapped)
    return attended, query_gradient, token_grad, key_weight_grad, value_weight_grad


def solution(mesh):
    split = P("ctx", "tp")
    in_specs = (P("ctx", None), P("ctx"), P(), split, split, split, split)
    return jax.shard_map(
        local, mesh=mesh, in_specs=in_specs, out_specs=(split,) * 5, check_vma=False
    )
```
